32 devices in a mesh: dom: 8 (over z, y), ka: 4 (over x, core).
Axes of the slice: x: 2, y: 2, z: 4, core: 2. Of those that a mesh axis runs over, the one named last changes fastest.
Arguments:
- density: bfloat16 [64, 16, 64, 64], P('dom', 'ka'), as said below
- columns: int32 [64, 16], replicated, may hold values from 0 to 63, as said below
- live: int32 [64], replicated, may hold values from 1 to 16, as said below
Outputs:
- new_density: bfloat16 [64, 16, 64, 64], P('dom', 'ka')
The draws below stay inside these ranges and needn't reach their ends.
Inputs may be any that keep to these rules, and one draw needn't show every extreme that they name: columns[i, 0] = i and columns[i, 1] = i - 1 (cyclically over 64); the 16 entries of a block row are distinct and name block rows of domains at most two away from the domain i // 8 of row i, cyclically over the domains. Domains differ in how many of their slots are live. `density`: slot 0 of every block row holds its diagonal block.
All inputs are finite; a program needn't handle non-finite values.
Results may differ from the reference program's by a relative error of at most 0.019.
Values may be sent and summed in bfloat16 or wider, within the bound.
A program may use at most 64 MiB of HBM per device.

```python
import math
import jax
import jax.numpy as jnp
from jax import lax

BLOCK = 64
NB = 16
ROWS_DEV = 8
ROWS = 64
N_KA = 4


def draw_density(key, part):
    shape = (ROWS, NB, BLOCK, BLOCK)
    scale = 1.5 / math.sqrt(BLOCK * NB)
    first_key = jax.random.fold_in(jax.random.fold_in(key, 5), 0)
    base = jax.random.normal(first_key, shape, jnp.float32)
    identity = jnp.eye(BLOCK, dtype=jnp.float32)
    diagonal_slot = jnp.zeros((NB, 1, 1), jnp.float32).at[0].set(0.5)
    return (base * scale + diagonal_slot * identity).astype(jnp.bfloat16)


def draw_columns(key, part):
    row_ids = jnp.arange(ROWS, dtype=jnp.int32)
    local_pos = row_ids % ROWS_DEV

    def per_row(row_key, position):
        order = jax.random.permutation(row_key, 5 * ROWS_DEV - 2)
        picks = order[:NB - 2].astype(jnp.int32)
        skipped = 2 * ROWS_DEV + position - 1
        return picks + 2 * (picks >= skipped).astype(jnp.int32)
    row_keys = jax.random.split(jax.random.fold_in(key, 11), ROWS)
    offsets = jax.vmap(per_row)(row_keys, local_pos)
    window_start = (row_ids // ROWS_DEV - 2) * ROWS_DEV
    others = jnp.mod(window_start[:, None] + offsets, ROWS)
    leading = jnp.stack([row_ids, jnp.mod(row_ids - 1, ROWS)], axis=1)
    return jnp.concatenate([leading, others], axis=1).astype(jnp.int32)


def draw_live(key, part):
    first_key, second_key = jax.random.split(jax.random.fold_in(key, 23))
    levels = jax.random.randint(first_key, (ROWS // ROWS_DEV,), 1, 5)
    level_row = jnp.repeat(levels, ROWS_DEV)
    lowest = jnp.maximum(level_row * NB // 8, 1)
    highest = level_row * NB // 4 + 1
    draws = jax.random.randint(second_key, (ROWS,), 0, 1 << 20)
    counts = lowest + draws % (highest - lowest)
    counts = jnp.minimum(counts, NB).at[0].set(NB)
    return counts.astype(jnp.int32)


def setup_inputs(seed: int = 0) -> dict:
    seeds = jax.random.split(jax.random.key(seed), 4)
    density = draw_density(jax.random.fold_in(seeds[3], 71), 0)
    columns = draw_columns(jax.random.fold_in(seeds[3], 71), 0)
    live = draw_live(jax.random.fold_in(seeds[3], 71), 0)
    return {"density": density, "columns": columns, "live": live}


def product_rows(left_blocks, row_cols, density, columns, live):
    slot_ids = jnp.arange(NB, dtype=jnp.int32)
    right_blocks = density[row_cols]
    inner_pattern = columns[row_cols]
    inner_live = live[row_cols]
    matches = (inner_pattern[:, None, :] == row_cols[None, :, None]) & (slot_ids[None, None, :] < inner_live[:, None, None])
    where_at = jnp.sum(jnp.where(matches, slot_ids[None, None, :], 0), axis=2).astype(jnp.int32)
    located = jnp.any(matches, axis=2)
    picked = right_blocks[slot_ids[:, None], where_at]
    picked = jnp.where(located[:, :, None, None], picked, jnp.zeros((), picked.dtype))
    quarter = NB // N_KA
    left_group = left_blocks.astype(jnp.float32).reshape(N_KA, quarter, BLOCK, BLOCK)
    picked_group = picked.astype(jnp.float32).reshape(N_KA, quarter, NB, BLOCK, BLOCK)
    partial_sums = jnp.einsum('qtab,qtsbc->qsac', left_group, picked_group)
    rounded = lax.optimization_barrier(partial_sums.astype(jnp.bfloat16)).astype(jnp.float32)
    return jnp.sum(rounded, axis=0)


def reference(density, columns, live):
    slot_ids = jnp.arange(NB, dtype=jnp.int32)

    def per_row(row_index):
        row_cols = columns[row_index]
        valid = (slot_ids < live[row_index])[:, None, None]
        left_blocks = jnp.where(valid, density[row_index], jnp.zeros((), jnp.bfloat16))
        square_sum = jnp.where(valid, product_rows(left_blocks, row_cols, density, columns, live), jnp.float32(0.0))
        square_low = square_sum.astype(jnp.bfloat16)
        cube_sum = jnp.where(valid, product_rows(square_low, row_cols, density, columns, live), jnp.float32(0.0))
        return (3.0 * square_sum - 2.0 * cube_sum).astype(jnp.bfloat16)

    return lax.map(per_row, jnp.arange(ROWS, dtype=jnp.int32))
```

```python
import functools

import jax
import jax.numpy as jnp
from jax import lax
from jax.experimental import pallas as pl
from jax.experimental.pallas import tpu as pltpu
from jax.sharding import PartitionSpec as P

MESH = pl.DeviceIdType.MESH
BF = jnp.bfloat16
F32 = jnp.float32
REACH = (0, 1, -1, 2, -2)


def iota(shape, dim):
    return lax.broadcasted_iota(jnp.int32, shape, dim)


def dot(a, b):
    return jnp.dot(a, b, preferred_element_type=F32)


def exact_dot(a, b):
    return dot(a, b).astype(BF)


def onehot(cond):
    return jnp.where(cond, F32(1), F32(0)).astype(BF)


def permutation(source, target):
    sizes = {"h": 2, "k": 4, "u": 4}
    lane = iota((512, 1), 0)
    digits, rest = {}, lane // 16
    for name in reversed(source):
        digits[name] = rest % sizes[name]
        rest = rest // sizes[name]
    place = jnp.zeros_like(lane)
    for name in target:
        place = place * sizes[name] + digits[name]
    place = place * 16 + lane % 16
    return onehot(jnp.broadcast_to(place, (512, 512)) == iota((512, 512), 1))


def kernel(
    ndom, rows_total, live_ref, density_ref, columns_ref, out_ref,
    a_buf, pieces, zin, win, left_in, square_in, square_own, new_pieces, yin,
    expand, gather, ldense, ddense, total, square_f32, mask_buf, rel_buf,
    send_a, recv_a, send_w, recv_w, send_l, recv_l, send_s, recv_s, send_n, recv_n,
):
    dom, ka = lax.axis_index("dom"), lax.axis_index("ka")

    def near(shift):
        return lax.rem(dom + shift + ndom, ndom)

    def peer(shift):
        return lax.rem(ka + shift, 4)

    barrier = pltpu.get_barrier_semaphore()
    for shift in REACH[1:]:
        pl.semaphore_signal(barrier, inc=1, device_id=(near(shift), ka), device_id_type=MESH)
    for shift in (1, 2, 3):
        pl.semaphore_signal(barrier, inc=1, device_id=(dom, peer(shift)), device_id_type=MESH)

    for i in range(4):
        for h in range(2):
            for u in range(4):
                at = (h * 4 + u) * 64
                a_buf[i * 64:(i + 1) * 64, at:at + 64] = density_ref[h * 4 + i, u]
    packed = exact_dot(a_buf[...], permutation("huk", "khu"))
    for k in range(4):
        pieces[k] = packed[:, k * 128:(k + 1) * 128]
    zin[ka] = pieces[ka]

    pl.semaphore_wait(barrier, 7)

    def spread(src_of, dst, send, recv):
        copies = []
        for shift in (2, 3, 1):
            to = peer(shift)
            copies.append(pltpu.make_async_remote_copy(
                src_ref=src_of(to), dst_ref=dst.at[ka],
                send_sem=send.at[shift - 1], recv_sem=recv.at[shift - 1],
                device_id=(dom, to), device_id_type=MESH))
        for copy in copies:
            copy.start()
        return copies

    copies_a = spread(lambda to: pieces.at[to], zin, send_a, recv_a)

    first_row = lax.rem((dom - 2 + ndom) * 8, rows_total)
    slot = iota((8, 16), 1)
    for o in range(5):
        base = pl.multiple_of(near(o - 2) * 8, 8)
        cols = columns_ref[pl.ds(base, 8), :]
        rel = cols - first_row
        rel = jnp.where(rel < 0, rel + rows_total, rel)
        row = iota((8, 16), 0)
        count = jnp.zeros((8, 16), jnp.int32)
        for r in range(8):
            count = jnp.where(row == r, live_ref[base + r], count)
        keep = (slot < count) & (rel < 40)
        rel_buf[o * 8:(o + 1) * 8, :] = jnp.where(keep, rel, -64).astype(F32)
    rel_all = rel_buf[...].astype(BF)
    repeat = onehot(iota((256, 16), 0) // 16 == iota((256, 16), 1))
    target = lax.dot_general(repeat, rel_all, (((1,), (1,)), ((), ())), preferred_element_type=F32)
    target = target * 16.0 + (iota((256, 40), 0) % 16).astype(F32)
    target_own = lax.dot_general(rel_all[16:24], repeat, (((1,), (1,)), ((), ())), preferred_element_type=F32)
    target_own = target_own * 16.0 + (iota((8, 256), 1) % 16).astype(F32)

    def build(o):
        lane = iota((256, 640), 1).astype(F32)
        for r in range(8):
            n = o * 8 + r
            expand[n] = onehot(jnp.broadcast_to(target[:, n:n + 1], (256, 640)) == lane)

    build(2)
    place = iota((640, 256), 0).astype(F32)
    for r in range(8):
        gather[r] = onehot(jnp.broadcast_to(target_own[r:r + 1, :], (640, 256)) == place)

    for copy in copies_a:
        copy.wait_recv()
    z = jnp.concatenate([zin[k] for k in range(4)], axis=1)
    mine = exact_dot(z, permutation("khu", "hku"))
    win[2, 0:256, :] = mine[:, 0:256]
    win[2, 256:512, :] = mine[:, 256:512]
    left_in[ka] = win[2]

    copies_w = {}
    for n, shift in enumerate((2, -2, 1, -1)):
        copies_w[shift] = pltpu.make_async_remote_copy(
            src_ref=win.at[2], dst_ref=win.at[2 - shift],
            send_sem=send_w.at[n], recv_sem=recv_w.at[n],
            device_id=(near(shift), ka), device_id_type=MESH)
        copies_w[shift].start()
    copies_l = spread(lambda to: win.at[2], left_in, send_l, recv_l)

    for o in (0, 1, 3, 4):
        build(o)
    for r in range(8):
        hit = jnp.max(expand[16 + r].astype(F32), axis=0, keepdims=True)
        mask_buf[r:r + 1, :] = hit

    def expand_window(o):
        def step(r, _):
            d = exact_dot(win[o, pl.ds(pl.multiple_of(r * 64, 64), 64), :], expand[o * 8 + r])
            for k in range(4):
                at = pl.multiple_of(o * 512 + k * 128 + r * 16, 16)
                ddense[pl.ds(at, 16), :] = d[k * 16:(k + 1) * 16, :]
            return 0
        lax.fori_loop(0, 8, step, 0)

    def expand_left(src):
        def step(r, _):
            rows = pl.ds(pl.multiple_of(r * 64, 64), 64)
            x = jnp.concatenate([src[k, rows, :] for k in range(4)], axis=0)
            d = exact_dot(x, expand[16 + r])
            for k in range(4):
                for o in range(5):
                    ldense[rows, o * 512 + k * 128:o * 512 + (k + 1) * 128] = (
                        d[k * 64:(k + 1) * 64, o * 128:(o + 1) * 128])
            return 0
        lax.fori_loop(0, 8, step, 0)

    expand_window(2)
    for copy in copies_l:
        copy.wait_recv()
    expand_left(left_in)
    square_f32[...] = dot(ldense[:, 1024:1536], ddense[1024:1536, :])
    for shift in (1, -1, 2, -2):
        o = 2 - shift
        copies_w[shift].wait_recv()
        expand_window(o)
        square_f32[...] += dot(ldense[:, o * 512:(o + 1) * 512], ddense[o * 512:(o + 1) * 512, :])

    def pick(value, r):
        kept = jnp.where(mask_buf[pl.ds(r, 1), :] > 0.5, value, F32(0))
        return exact_dot(kept.astype(BF), gather[r])

    for r in range(8):
        rows = slice(r * 64, (r + 1) * 64)
        square_own[rows, :] = pick(square_f32[rows, :], r)
    square_in[ka] = square_own[...]
    copies_s = spread(lambda to: square_own, square_in, send_s, recv_s)
    for copy in copies_s:
        copy.wait_recv()
    expand_left(square_in)
    total[...] = 3.0 * square_f32[...] - 2.0 * dot(ldense[...], ddense[...])
    news = []
    for r in range(8):
        news.append(pick(total[r * 64:(r + 1) * 64, :], r))
    new = jnp.concatenate(
        [jnp.concatenate(news[:4], axis=0), jnp.concatenate(news[4:], axis=0)], axis=1)
    packed = exact_dot(new, permutation("hku", "khu"))
    for k in range(4):
        new_pieces[k] = packed[:, k * 128:(k + 1) * 128]
    yin[ka] = new_pieces[ka]
    copies_n = spread(lambda to: new_pieces.at[to], yin, send_n, recv_n)
    back = permutation("khu", "huk")
    for copy in copies_n:
        copy.wait_recv()
    y = exact_dot(jnp.concatenate([yin[k] for k in range(4)], axis=1), back)
    for i in range(4):
        for h in range(2):
            for u in range(4):
                at = (h * 4 + u) * 64
                out_ref[h * 4 + i, u] = y[i * 64:(i + 1) * 64, at:at + 64]
    for copies in (copies_a, copies_l, copies_s, copies_n, list(copies_w.values())):
        for copy in copies:
            copy.wait_send()


def shards(density, columns, live):
    rows_total = columns.shape[0]
    dma = pltpu.SemaphoreType.DMA
    vmem = pltpu.VMEM
    return pl.pallas_call(
        functools.partial(kernel, lax.axis_size("dom"), rows_total),
        out_shape=jax.ShapeDtypeStruct(density.shape, BF),
        in_specs=[
            pl.BlockSpec(memory_space=pltpu.SMEM),
            pl.BlockSpec(memory_space=pltpu.VMEM),
            pl.BlockSpec(memory_space=pltpu.VMEM),
        ],
        out_specs=pl.BlockSpec(memory_space=pltpu.VMEM),
        scratch_shapes=[
            vmem((256, 512), BF),
            vmem((4, 256, 128), BF),
            vmem((4, 256, 128), BF),
            vmem((5, 512, 256), BF),
            vmem((4, 512, 256), BF),
            vmem((4, 512, 256), BF),
            vmem((512, 256), BF),
            vmem((4, 256, 128), BF),
            vmem((4, 256, 128), BF),
            vmem((40, 256, 640), BF),
            vmem((8, 640, 256), BF),
            vmem((512, 2560), BF),
            vmem((2560, 640), BF),
            vmem((512, 640), F32),
            vmem((512, 640), F32),
            vmem((8, 640), F32),
            vmem((40, 16), F32),
            dma((3,)), dma((3,)), dma((4,)), dma((4,)), dma((3,)), dma((3,)),
            dma((3,)), dma((3,)), dma((3,)), dma((3,)),
        ],
        compiler_params=pltpu.CompilerParams(
            collective_id=0, has_side_effects=True, vmem_limit_bytes=56 * 1024 * 1024),
    )(live, density, columns)


def solution(mesh):
    return jax.shard_map(
        shards,
        mesh=mesh,
        in_specs=(P("dom", "ka", None, None), P(), P()),
        out_specs=P("dom", "ka", None, None),
        check_vma=False,
    )
```

```python
import functools

import jax
import jax.numpy as jnp
from jax import lax
from jax.experimental import pallas as pl
from jax.experimental.pallas import tpu as pltpu
from jax.sharding import PartitionSpec as P

MESH = pl.DeviceIdType.MESH
BF = jnp.bfloat16
F32 = jnp.float32
CHUNKS = 4


def iota(shape, dim):
    return lax.broadcasted_iota(jnp.int32, shape, dim)


def dot(a, b):
    return jnp.dot(a, b, preferred_element_type=F32)


def exact_dot(a, b):
    return dot(a, b).astype(BF)


def onehot(cond):
    return jnp.where(cond, F32(1), F32(0)).astype(BF)


def permutation(source, target):
    sizes = {"h": 2, "k": 4, "u": 4}
    lane = iota((512, 1), 0)
    digits, rest = {}, lane // 16
    for name in reversed(source):
        digits[name] = rest % sizes[name]
        rest = rest // sizes[name]
    place = jnp.zeros_like(lane)
    for name in target:
        place = place * sizes[name] + digits[name]
    place = place * 16 + lane % 16
    return onehot(jnp.broadcast_to(place, (512, 512)) == iota((512, 512), 1))


class Gather:
    def __init__(self, ref, send, recv, dom, ka):
        flip = ka + 1 - 2 * lax.rem(ka, 2)
        across = lax.rem(ka + 2, 4)

        def copy(quarter, to, n, part):
            rows = pl.ds(part * 128, 128)
            return pltpu.make_async_remote_copy(
                src_ref=ref.at[quarter, rows], dst_ref=ref.at[quarter, rows],
                send_sem=send.at[n, part], recv_sem=recv.at[n, part],
                device_id=(dom, to), device_id_type=MESH)

        self.far = [copy(ka, across, 0, c) for c in range(CHUNKS)]
        self.close = [copy(ka, flip, 1, c) for c in range(CHUNKS)]
        self.passed = [copy(across, flip, 2, c) for c in range(CHUNKS)]

    def start(self, part):
        self.far[part].start()
        self.close[part].start()

    def forward(self, part):
        self.far[part].wait_recv()
        self.passed[part].start()

    def wait_part(self, part):
        self.close[part].wait_recv()
        self.passed[part].wait_recv()

    def wait(self):
        for part in range(CHUNKS):
            self.wait_part(part)

    def finish(self):
        for copy in self.far + self.close + self.passed:
            copy.wait_send()


def kernel(
    ndom, rows_total, live_ref, density_ref, columns_ref, out_ref,
    a_buf, pieces, zin, win, left_in, square_in, new_pieces, yin,
    expand, gather, ldense, ddense, total, square_f32, mask_buf, rel_buf,
    send_a, recv_a, send_w, recv_w, send_l, recv_l, send_s, recv_s, send_n, recv_n,
):
    dom, ka = lax.axis_index("dom"), lax.axis_index("ka")

    def near(shift):
        return lax.rem(dom + shift + ndom, ndom)

    def peer(shift):
        return lax.rem(ka + shift, 4)

    barrier = pltpu.get_barrier_semaphore()
    side = 1 - 2 * lax.rem(dom, 2)
    for to in (near(2), near(-2), near(side)):
        pl.semaphore_signal(barrier, inc=1, device_id=(to, ka), device_id_type=MESH)
    for shift in (1, 2, 3):
        pl.semaphore_signal(barrier, inc=1, device_id=(dom, peer(shift)), device_id_type=MESH)

    for i in range(4):
        for h in range(2):
            for u in range(4):
                at = (h * 4 + u) * 64
                a_buf[i * 64:(i + 1) * 64, at:at + 64] = density_ref[h * 4 + i, u]
    packed = exact_dot(a_buf[...], permutation("huk", "khu"))
    for k in range(4):
        pieces[k] = packed[:, k * 128:(k + 1) * 128]
    zin[ka] = pieces[ka]

    pl.semaphore_wait(barrier, 6)

    def spread(src_of, dst, send, recv):
        copies = []
        for shift in (2, 3, 1):
            to = peer(shift)
            copies.append(pltpu.make_async_remote_copy(
                src_ref=src_of(to), dst_ref=dst.at[ka],
                send_sem=send.at[shift - 1], recv_sem=recv.at[shift - 1],
                device_id=(dom, to), device_id_type=MESH))
        for copy in copies:
            copy.start()
        return copies

    copies_a = spread(lambda to: pieces.at[to], zin, send_a, recv_a)

    first_row = lax.rem((dom - 2 + ndom) * 8, rows_total)
    slot = iota((8, 16), 1)
    for o in range(5):
        base = pl.multiple_of(near(o - 2) * 8, 8)
        cols = columns_ref[pl.ds(base, 8), :]
        rel = cols - first_row
        rel = jnp.where(rel < 0, rel + rows_total, rel)
        row = iota((8, 16), 0)
        count = jnp.zeros((8, 16), jnp.int32)
        for r in range(8):
            count = jnp.where(row == r, live_ref[base + r], count)
        keep = (slot < count) & (rel < 40)
        rel_buf[o * 8:(o + 1) * 8, :] = jnp.where(keep, rel, -64).astype(F32)
    rel_all = rel_buf[...].astype(BF)
    repeat = onehot(iota((256, 16), 0) // 16 == iota((256, 16), 1))
    target = lax.dot_general(repeat, rel_all, (((1,), (1,)), ((), ())), preferred_element_type=F32)
    target = target * 16.0 + (iota((256, 40), 0) % 16).astype(F32)
    target_own = lax.dot_general(rel_all[16:24], repeat, (((1,), (1,)), ((), ())), preferred_element_type=F32)
    target_own = target_own * 16.0 + (iota((8, 256), 1) % 16).astype(F32)

    def build(o):
        lane = iota((256, 640), 1).astype(F32)
        for r in range(8):
            n = o * 8 + r
            expand[n] = onehot(jnp.broadcast_to(target[:, n:n + 1], (256, 640)) == lane)

    build(2)
    place = iota((640, 256), 0).astype(F32)
    for r in range(8):
        gather[r] = onehot(jnp.broadcast_to(target_own[r:r + 1, :], (640, 256)) == place)

    for copy in copies_a:
        copy.wait_recv()
    z = jnp.concatenate([zin[k] for k in range(4)], axis=1)
    mine = exact_dot(z, permutation("khu", "hku"))
    win[2, 0:256, :] = mine[:, 0:256]
    win[2, 256:512, :] = mine[:, 256:512]
    left_in[ka] = win[2]

    def to_dom(src, dst, part, to, n):
        rows = pl.ds(part * 128, 128)
        return pltpu.make_async_remote_copy(
            src_ref=win.at[src, rows], dst_ref=win.at[dst, rows],
            send_sem=send_w.at[n, part], recv_sem=recv_w.at[n, part],
            device_id=(to, ka), device_id_type=MESH)

    parts = range(CHUNKS)
    up = [to_dom(2, 0, c, near(2), 0) for c in parts]
    down = [to_dom(2, 4, c, near(-2), 1) for c in parts]
    beside = [to_dom(2, 2 - side, c, near(side), 2) for c in parts]
    passed = [to_dom(2 + 2 * side, 2 + side, c, near(side), 3) for c in parts]
    left = Gather(left_in, send_l, recv_l, dom, ka)
    for c in parts:
        up[c].start()
        down[c].start()
        left.start(c)
        beside[c].start()

    def pass_window(c):
        up[c].wait_recv()
        down[c].wait_recv()
        passed[c].start()

    build(0)
    left.forward(0)
    build(1)
    left.forward(1)
    pass_window(0)
    build(3)
    left.forward(2)
    build(4)
    left.forward(3)
    pass_window(1)
    for r in range(8):
        hit = jnp.max(expand[16 + r].astype(F32), axis=0, keepdims=True)
        mask_buf[r:r + 1, :] = hit

    def expand_window(o):
        for r in range(8):
            d = exact_dot(win[o, r * 64:(r + 1) * 64, :], expand[o * 8 + r])
            for k in range(4):
                at = pl.multiple_of(o * 512 + k * 128 + r * 16, 16)
                ddense[pl.ds(at, 16), :] = d[k * 16:(k + 1) * 16, :]

    def expand_left(src, r):
        rows = slice(r * 64, (r + 1) * 64)
        x = jnp.concatenate([src[k, rows, :] for k in range(4)], axis=0)
        d = exact_dot(x, expand[16 + r])
        for k in range(4):
            for o in range(5):
                ldense[rows, o * 512 + k * 128:o * 512 + (k + 1) * 128] = (
                    d[k * 64:(k + 1) * 64, o * 128:(o + 1) * 128])

    def product(o):
        at = pl.ds(pl.multiple_of(o * 512, 512), 512)
        return dot(ldense[:, at], ddense[at, :])

    expand_window(2)
    left.wait()
    for r in range(8):
        expand_left(left_in, r)
    pass_window(2)
    square_f32[...] = product(2)
    for copy in beside:
        copy.wait_recv()
    expand_window(2 + side)
    square_f32[...] += product(2 + side)
    pass_window(3)
    for o in (0, 4):
        expand_window(o)
        square_f32[...] += product(o)
    for copy in passed:
        copy.wait_recv()
    expand_window(2 - side)
    square_f32[...] += product(2 - side)

    def pick(value, r):
        kept = jnp.where(mask_buf[pl.ds(r, 1), :] > 0.5, value, F32(0))
        return exact_dot(kept.astype(BF), gather[r])

    squares = Gather(square_in, send_s, recv_s, dom, ka)
    for c in parts:
        for r in (2 * c, 2 * c + 1):
            rows = slice(r * 64, (r + 1) * 64)
            square_in[ka, rows, :] = pick(square_f32[rows, :], r)
        squares.start(c)
    for c in parts:
        squares.forward(c)
    turn, back = permutation("hku", "khu"), permutation("khu", "huk")
    for c in parts:
        squares.wait_part(c)
        expand_left(square_in, 2 * c)
        expand_left(square_in, 2 * c + 1)
    total[...] = 3.0 * square_f32[...] - 2.0 * dot(ldense[...], ddense[...])
    news = []
    for r in range(8):
        news.append(pick(total[r * 64:(r + 1) * 64, :], r))
    new = jnp.concatenate(
        [jnp.concatenate(news[:4], axis=0), jnp.concatenate(news[4:], axis=0)], axis=1)
    packed = exact_dot(new, turn)
    for k in range(4):
        new_pieces[k] = packed[:, k * 128:(k + 1) * 128]
    yin[ka] = new_pieces[ka]
    copies_n = spread(lambda to: new_pieces.at[to], yin, send_n, recv_n)
    for copy in copies_n:
        copy.wait_recv()
    y = exact_dot(jnp.concatenate([yin[k] for k in range(4)], axis=1), back)
    for i in range(4):
        for h in range(2):
            for u in range(4):
                at = (h * 4 + u) * 64
                out_ref[h * 4 + i, u] = y[i * 64:(i + 1) * 64, at:at + 64]
    for copies in (copies_a, copies_n, up, down, beside, passed):
        for copy in copies:
            copy.wait_send()
    left.finish()
    squares.finish()


def shards(density, columns, live):
    rows_total = columns.shape[0]
    dma = pltpu.SemaphoreType.DMA
    vmem = pltpu.VMEM
    return pl.pallas_call(
        functools.partial(kernel, lax.axis_size("dom"), rows_total),
        out_shape=jax.ShapeDtypeStruct(density.shape, BF),
        in_specs=[
            pl.BlockSpec(memory_space=pltpu.SMEM),
            pl.BlockSpec(memory_space=pltpu.VMEM),
            pl.BlockSpec(memory_space=pltpu.VMEM),
        ],
        out_specs=pl.BlockSpec(memory_space=pltpu.VMEM),
        scratch_shapes=[
            vmem((256, 512), BF),
            vmem((4, 256, 128), BF),
            vmem((4, 256, 128), BF),
            vmem((5, 512, 256), BF),
            vmem((4, 512, 256), BF),
            vmem((4, 512, 256), BF),
            vmem((4, 256, 128), BF),
            vmem((4, 256, 128), BF),
            vmem((40, 256, 640), BF),
            vmem((8, 640, 256), BF),
            vmem((512, 2560), BF),
            vmem((2560, 640), BF),
            vmem((512, 640), F32),
            vmem((512, 640), F32),
            vmem((8, 640), F32),
            vmem((40, 16), F32),
            dma((3,)), dma((3,)), dma((4, CHUNKS)), dma((4, CHUNKS)),
            dma((3, CHUNKS)), dma((3, CHUNKS)), dma((3, CHUNKS)), dma((3, CHUNKS)),
            dma((3,)), dma((3,)),
        ],
        compiler_params=pltpu.CompilerParams(
            collective_id=0, has_side_effects=True, vmem_limit_bytes=56 * 1024 * 1024),
    )(live, density, columns)


def solution(mesh):
    return jax.shard_map(
        shards,
        mesh=mesh,
        in_specs=(P("dom", "ka", None, None), P(), P()),
        out_specs=P("dom", "ka", None, None),
        check_vma=False,
    )
```
